256 devices in a mesh: orb: 8 (over y_hi, x), pt: 32 (over y_lo, z, core).
Axes of the slice: x: 4, y: 4 (y_hi: 2, y_lo: 2; y = y_hi * 2 + y_lo), z: 8, core: 2. Of those that a mesh axis runs over, the one named last changes fastest.
Arguments:
- collocation: bfloat16 [2048, 49152], P('orb', 'pt'), may hold values from -0.8984375 to 0.8984375
- pair_tensor: bfloat16 [49152, 128], P('pt'), may hold values from -0.02734375 to 0.02734375
Outputs:
- fitted: float32 [4096, 128], P(('orb', 'pt'))
The draws below stay inside these ranges and needn't reach their ends.
All inputs are finite; a program needn't handle non-finite values.
Results may differ from the reference program's by a relative error of at most 0.0034.
Values may be sent and summed in bfloat16 or wider, within the bound.
No kernel may reach another device: no remote copies, remote signals or barrier semaphores. Data moves between devices by JAX's collectives and lax.ppermute only.
A program may use at most 128 MiB of HBM per device.

```python
import jax
import jax.numpy as jnp
from jax import lax

NORB = 2048
AUX = 128
PTS_DEV = 1536
PAN_DEV = 128
NPTS = 49152
PANEL = 4096
N_PT = 32


def level_of(rng, dims, cuts, smallest, top_value):
    def one(position, shards_of):
        steps = jax.random.uniform(jax.random.fold_in(jax.random.fold_in(rng, 6), position), (shards_of,), jnp.float32, smallest / len(cuts), top_value / len(cuts))
        return jnp.repeat(jnp.exp(steps), dims[position] // shards_of).reshape((-1,) + (1,) * (len(dims) - position - 1))

    factor_of = one(*cuts[0])
    for cut in cuts[1:]:
        factor_of = factor_of * one(*cut)
    return factor_of


def bell_draw(key, dims, scale, limit, pieces=(), dtype=jnp.bfloat16):
    result = jax.random.normal(key, dims, jnp.float32) * scale
    if len(pieces) > 0:
        result = level_of(key, dims, pieces, -0.22, 0.18) * result
    return jnp.clip(result, min=-limit, max=limit).astype(dtype)


def setup_inputs(seed: int = 0) -> dict:
    splits = jax.random.split(jax.random.key(seed), 3)
    return {
        "collocation": bell_draw(splits[0], (NORB, NPTS), 0.15, 0.8984375, ((0, 8), (1, 32))),
        "pair_tensor": bell_draw(splits[1], (NPTS, AUX), NPTS ** -0.5, 0.02734375, ((0, 32),)),
    }


def reference(collocation, pair_tensor):
    selected = collocation.reshape(NORB, N_PT, PTS_DEV)[:, :, :PAN_DEV]
    panel_blocks = jnp.transpose(selected, (1, 0, 2))

    def fit_block(block):
        gram_block = lax.dot_general(block, collocation, (((0,), (0,)), ((), ())), preferred_element_type=jnp.float32)
        squared = (gram_block * gram_block).astype(jnp.bfloat16)
        return jnp.dot(squared, pair_tensor, preferred_element_type=jnp.float32)

    fitted = lax.map(fit_block, panel_blocks)
    return fitted.reshape(PANEL, AUX)
```

```python
import jax
import jax.numpy as jnp
import numpy as np
from jax import lax
from jax.sharding import Mesh, PartitionSpec as P

PAN_DEV = 128
AXES = ("yh", "x", "yl", "z", "c")
SIZES = (2, 4, 2, 8, 2)


def perm_of(move, only=lambda yh, x, yl, z, c: True):
    pairs = []
    for s in range(256):
        at = tuple(int(i) for i in np.unravel_index(s, SIZES))
        if only(*at):
            to = tuple(i % n for i, n in zip(move(*at), SIZES))
            pairs.append((s, int(np.ravel_multi_index(to, SIZES))))
    return pairs


def x_shift(d):
    return perm_of(lambda yh, x, yl, z, c: (yh, x + d, yl, z, c))


def z_shift(d):
    return perm_of(lambda yh, x, yl, z, c: (yh, x, yl, z + d, c))


CORE = perm_of(lambda yh, x, yl, z, c: (yh, x, yl, z, 1 - c))
Y_LO = perm_of(lambda yh, x, yl, z, c: (yh, x, 1 - yl, z, c))
Y_HI = perm_of(lambda yh, x, yl, z, c: (1 - yh, x, yl, z, c))
Y_BOTH = perm_of(lambda yh, x, yl, z, c: (1 - yh, x, 1 - yl, z, c))
TRADE = perm_of(lambda yh, x, yl, z, c: (1 - yh, x, yl, z, 1 - c), lambda yh, x, yl, z, c: c != yh)
SPREAD = perm_of(lambda yh, x, yl, z, c: (yh, z // 2, yl, 2 * x + z % 2, c))
SPREAD_CROSS = perm_of(lambda yh, x, yl, z, c: (yh, z // 2, yl, 2 * x + z % 2, 1 - c))


def send(a, perm):
    return lax.ppermute(a, AXES, perm)


def picker():
    m = np.zeros((2, 2, 4, 2, 16, 2, 4, 16), np.float32)
    for c in range(2):
        for src in range(2):
            for jj in range(4):
                for i in range(16):
                    m[c, src, jj, c, i, src, jj, i] = 1
    return m.reshape(2, 256, 128)


def on_device(collocation, pair_tensor):
    yh, x, yl, z, c = (lax.axis_index(a) for a in AXES)
    local_panel = collocation[:, :PAN_DEV]
    same, cross = send(local_panel, SPREAD), send(local_panel, SPREAD_CROSS)
    traded = send(collocation, TRADE)
    pair_cross = send(pair_tensor, CORE)

    pick = jnp.asarray(picker(), jnp.bfloat16)
    first = jnp.where(c == 0, same, cross)
    second = jnp.where(c == 0, cross, same)
    block = jnp.dot(
        jnp.concatenate([first, second], axis=1), pick[c], preferred_element_type=jnp.float32
    ).astype(jnp.bfloat16)

    ring = jnp.stack([block] + [send(block, z_shift(-d)) for d in range(1, 8)])
    ring = jnp.concatenate([ring, ring])
    ring = lax.dynamic_slice_in_dim(ring, lax.rem(2 * x - z + 8, 8), 8)
    slab = ring.reshape(4, 2, 256, 128).transpose(0, 2, 1, 3).reshape(1024, 256)
    lo, hi, both = send(slab, Y_LO), send(slab, Y_HI), send(slab, Y_BOTH)
    near = jnp.where(yl == 0, jnp.concatenate([slab, lo], 1), jnp.concatenate([lo, slab], 1))
    far = jnp.where(yl == 0, jnp.concatenate([hi, both], 1), jnp.concatenate([both, hi], 1))

    held = jnp.where(c == yh, collocation, traded)
    mine = jnp.concatenate([held] + [send(held, x_shift(-d)) for d in range(1, 4)])
    others = send(mine, CORE)

    def gram(panel, cols):
        return lax.dot_general(panel, cols, (((0,), (0,)), ((), ())), preferred_element_type=jnp.float32)

    on_near, on_far = jnp.where(c == yh, mine, others), jnp.where(c == yh, others, mine)
    gram_block = gram(jnp.concatenate([near, far]), jnp.concatenate([on_near, on_far]))
    squared = (gram_block * gram_block).astype(jnp.bfloat16)
    pair = jnp.where(c == yh, pair_tensor, pair_cross)
    part = jnp.dot(squared, pair, preferred_element_type=jnp.float32)
    parts = lax.all_to_all(part.reshape(32, 16, 128), ("yh", "yl", "z"), 0, 0)
    return parts.sum(0)


def solution(mesh):
    return jax.shard_map(
        on_device,
        mesh=Mesh(mesh.devices.reshape(SIZES), AXES),
        in_specs=(P(("yh", "x"), ("yl", "z", "c")), P(("yl", "z", "c"), None)),
        out_specs=P(AXES, None),
        check_vma=False,
    )
```

```python
import jax
import jax.numpy as jnp
import numpy as np
from jax import lax
from jax.experimental import pallas as pl
from jax.experimental.pallas import tpu as pltpu
from jax.sharding import Mesh, PartitionSpec as P

PAN_DEV = 128
AXES = ("yh", "x", "yl", "z", "c")
SIZES = (2, 4, 2, 8, 2)
TILE = 512


def perm_of(move, only=lambda yh, c: True):
    pairs = []
    for s in range(256):
        yh, x, yl, z, c = (int(i) for i in np.unravel_index(s, SIZES))
        if only(yh, c):
            x, y, z, c = move(x, 2 * yh + yl, z, c)
            y = y % 4
            pairs.append((s, int(np.ravel_multi_index((y // 2, x % 4, y % 2, z % 8, c), SIZES))))
    return pairs


def is_own(y, c):
    return c == y // 2


def own(yh, c):
    return c == yh


CORE = perm_of(lambda x, y, z, c: (x, y, z, 1 - c))
SPREAD = perm_of(lambda x, y, z, c: (z // 2, y, 2 * x + z % 2, c))
TRADE = perm_of(lambda x, y, z, c: (x, y, z, c) if is_own(y, c) else (x, y + 2, z, 1 - c))


def x_step(d):
    return perm_of(lambda x, y, z, c: (x + d if c == 0 else x - d, y, z, c))


def y_step(d):
    return perm_of(lambda x, y, z, c: (x, y + d if c == 0 else y - d, z, c))


def send(a, perm):
    return lax.ppermute(a, AXES, perm)


def picker():
    m = np.zeros((2, 2, 4, 2, 16, 2, 4, 16), np.float32)
    for c in range(2):
        for s in range(2):
            for j in range(4):
                for i in range(16):
                    m[c, s, j, c, i, c ^ s, j, i] = 1
    return m.reshape(2, 256, 128)


def tile_kernel(h0, h1, h2, h3, g0, g1, g2, g3, pair, cspair, y0, y1, y2, y3, out, blocks):
    yh, x, yl, c = (lax.axis_index(a) for a in ("yh", "x", "yl", "c"))
    side = 2 * c - 1
    for dy, ref in ((0, y0), (side, y1), (-side, y2), (2, y3)):
        blocks[lax.rem(2 * yh + yl + dy + 4, 4)] = ref[...]
    out[...] = jnp.zeros_like(out)

    @pl.loop(0, h0.shape[1] // TILE)
    def _(t):
        at = pl.ds(pl.multiple_of(t * TILE, TILE), TILE)
        gram = jnp.zeros((512, TILE), jnp.float32)
        for half, dx, cols in (
            (c, 0, h0), (c, side, h1), (c, -side, h2), (c, 2, h3),
            (1 - c, 0, g0), (1 - c, -side, g1), (1 - c, side, g2), (1 - c, 2, g3),
        ):
            rows = blocks[pl.ds(2 * half, 2), pl.ds(2 * lax.rem(x + dx + 4, 4), 2)].reshape(512, 256)
            gram += jnp.dot(rows, cols[:, at], preferred_element_type=jnp.float32)
        weights = jnp.where(c == yh, pair[at, :], cspair[at, :])
        out[...] += jnp.dot((gram * gram).astype(jnp.bfloat16), weights, preferred_element_type=jnp.float32)


def tile_product(*operands):
    return pl.pallas_call(
        tile_kernel,
        out_shape=jax.ShapeDtypeStruct((512, 128), jnp.float32),
        in_specs=[pl.BlockSpec(memory_space=pltpu.VMEM)] * len(operands),
        out_specs=pl.BlockSpec(memory_space=pltpu.VMEM),
        scratch_shapes=[pltpu.VMEM((4, 8, 128, 256), jnp.bfloat16)],
        compiler_params=pltpu.CompilerParams(vmem_limit_bytes=24 * 2**20),
        cost_estimate=pl.CostEstimate(flops=3_400_000_000, bytes_accessed=9_000_000, transcendentals=0),
    )(*operands)


def on_device(collocation, pair_tensor):
    c = lax.axis_index("c")

    h0 = send(collocation, TRADE)
    local_panel = send(collocation[:, :PAN_DEV], SPREAD)
    cspair = send(pair_tensor, CORE)

    both = jnp.concatenate([local_panel, send(local_panel, CORE)], axis=1)
    pick = lax.dynamic_index_in_dim(jnp.asarray(picker(), jnp.bfloat16), c, keepdims=False)
    block = lax.dot_general(
        pick, both, (((0,), (1,)), ((), ())), preferred_element_type=jnp.float32
    ).astype(jnp.bfloat16)
    block, h0 = lax.optimization_barrier((block, h0))
    ring = lax.all_to_all(jnp.broadcast_to(block[None], (8, 128, 256)), "z", 0, 0)

    h1, h2 = send(h0, x_step(1)), send(h0, x_step(-1))
    h = [h0, h1, h2, send(h1, x_step(1))]
    y1, y2 = send(ring, y_step(1)), send(ring, y_step(-1))
    g = [send(a, CORE) for a in h]
    part = tile_product(*h, *g, pair_tensor, cspair, ring, y1, y2, send(y1, y_step(1)))
    parts = lax.all_to_all(part.reshape(32, 16, 128), ("yh", "yl", "z"), 0, 0)
    return parts.sum(0)


def solution(mesh):
    return jax.shard_map(
        on_device,
        mesh=Mesh(mesh.devices.reshape(SIZES), AXES),
        in_specs=(P(("yh", "x"), ("yl", "z", "c")), P(("yl", "z", "c"), None)),
        out_specs=P(AXES, None),
        check_vma=False,
    )
```

```python
import jax
import jax.numpy as jnp
import numpy as np
from jax import lax
from jax.experimental import pallas as pl
from jax.experimental.pallas import tpu as pltpu
from jax.sharding import Mesh, PartitionSpec as P

PAN_DEV = 128
AXES = ("yh", "x", "yl", "z", "c")
SIZES = (2, 4, 2, 8, 2)
TILE = 512


def perm_of(move, only=lambda yh, c: True):
    pairs = []
    for s in range(256):
        yh, x, yl, z, c = (int(i) for i in np.unravel_index(s, SIZES))
        if only(yh, c):
            x, y, z, c = move(x, 2 * yh + yl, z, c)
            y = y % 4
            pairs.append((s, int(np.ravel_multi_index((y // 2, x % 4, y % 2, z % 8, c), SIZES))))
    return pairs


def is_own(y, c):
    return c == y // 2


def own(yh, c):
    return c == yh


CORE = perm_of(lambda x, y, z, c: (x, y, z, 1 - c))
SPREAD, SPREAD_FAR = (perm_of(lambda x, y, z, c: (z // 2, y, 2 * x + z % 2 + d, c)) for d in (0, 4))
TRADE = perm_of(lambda x, y, z, c: (x, y, z, c) if is_own(y, c) else (x, y + 2, z, 1 - c))


def x_step(d):
    return perm_of(lambda x, y, z, c: (x + d if c == 0 else x - d, y, z, c))


def z_step(d):
    return perm_of(lambda x, y, z, c: (x, y, z + d if c == 0 else z - d, c))


def y_step(d):
    return perm_of(lambda x, y, z, c: (x, y + d if c == 0 else y - d, z, c))


def send(a, perm):
    return lax.ppermute(a, AXES, perm)


def picker():
    m = np.zeros((2, 4, 2, 16, 2, 4, 16), np.float32)
    for c in range(2):
        for r in range(2):
            for j in range(4):
                for i in range(16):
                    m[c, j, c ^ r, i, r, j, i] = 1
    return m.reshape(2, 128, 128)


def place(blocks, ref, first=0):
    z, c = lax.axis_index("z"), lax.axis_index("c")
    side = 2 * c - 1
    for i in range(ref.shape[0]):
        off = (0, side, -side, 2 * side)[(first + i) // 2] + 4 * (i % 2)
        blocks[lax.rem(z + off + 8, 8)] = ref[i]


def first_kernel(h0, h1, h2, g0, g1, g2, *rest):
    *panel, out, blocks = rest
    yh, x, yl, c = (lax.axis_index(a) for a in ("yh", "x", "yl", "c"))
    side = 2 * c - 1
    for dy, ref in zip((0, side, -side), panel):
        place(blocks.at[lax.rem(2 * yh + yl + dy + 4, 4)], ref)

    def product(whole, partial, sign):
        @pl.loop(0, out.shape[1] // TILE)
        def _(t):
            at = pl.ds(pl.multiple_of(t * TILE, TILE), TILE)
            gram, more = 0, 0
            for dx, cols, others in zip((0, sign * side, -sign * side), whole, partial):
                z2 = 2 * lax.rem(x + dx + 4, 4)
                rows = blocks[pl.ds(2 * yh, 2), pl.ds(z2, 2)].reshape(512, 256)
                gram += jnp.dot(rows, cols[:, at], preferred_element_type=jnp.float32)
                z2 = 2 * lax.rem(x - dx + 4, 4)
                rows = blocks[2 * (1 - yh) + 1 - yl, pl.ds(z2, 2)].reshape(256, 256)
                more += jnp.dot(rows, others[:, at], preferred_element_type=jnp.float32)
            out[:, at] = gram
            out[pl.ds(pl.multiple_of((1 - yl) * 256, 256), 256), at] += more

    @pl.when(c == yh)
    def _():
        product((h0, h1, h2), (g0, g1, g2), 1)

    @pl.when(c != yh)
    def _():
        product((g0, g1, g2), (h0, h1, h2), -1)


def last_kernel(gram, blocks, h0, h1, h2, h3, g0, g1, g2, g3, pair, cspair, y3, y4, out, last):
    yh, x, yl, c = (lax.axis_index(a) for a in ("yh", "x", "yl", "c"))
    side = 2 * c - 1
    place(last, y3)
    place(last, y4, 4)
    out[...] = jnp.zeros_like(out)
    z2 = 2 * lax.rem(x + 2, 4)

    def product(whole, partial, weights, sign):
        @pl.loop(0, gram.shape[1] // TILE)
        def _(t):
            at = pl.ds(pl.multiple_of(t * TILE, TILE), TILE)
            here, there = (pl.ds(pl.multiple_of(r * 256, 256), 256) for r in (yl, 1 - yl))

            def add(values, rows, cols):
                return values + jnp.dot(rows.reshape(256, 256), cols[:, at], preferred_element_type=jnp.float32)

            def contract(rows, values):
                squared = (values * values).astype(jnp.bfloat16)
                out[rows, :] += jnp.dot(squared, weights[at, :], preferred_element_type=jnp.float32)

            values = add(gram[there, at], blocks[2 * yh + 1 - yl, pl.ds(z2, 2)], whole)
            contract(there, add(values, blocks[2 * (1 - yh) + 1 - yl, pl.ds(z2, 2)], partial[3]))
            values = add(gram[here, at], blocks[2 * yh + yl, pl.ds(z2, 2)], whole)
            for dx, cols in zip((0, sign * side, -sign * side, 2), partial):
                values = add(values, last[pl.ds(2 * lax.rem(x + dx + 4, 4), 2)], cols)
            contract(here, values)

    @pl.when(c == yh)
    def _():
        product(h3, (g0, g1, g2, g3), pair, -1)

    @pl.when(c != yh)
    def _():
        product(g3, (h0, h1, h2, h3), cspair, 1)


def call(kernel, shapes, scratch, flops, *operands):
    return pl.pallas_call(
        kernel,
        out_shape=[jax.ShapeDtypeStruct(*shape) for shape in shapes],
        in_specs=[pl.BlockSpec(memory_space=pltpu.VMEM)] * len(operands),
        out_specs=[pl.BlockSpec(memory_space=pltpu.VMEM)] * len(shapes),
        scratch_shapes=scratch,
        compiler_params=pltpu.CompilerParams(vmem_limit_bytes=24 * 2**20),
        cost_estimate=pl.CostEstimate(flops=flops, bytes_accessed=9_000_000, transcendentals=0),
    )(*operands)


def on_device(collocation, pair_tensor):
    c = lax.axis_index("c")

    pick = lax.dynamic_index_in_dim(jnp.asarray(picker(), jnp.bfloat16), c, keepdims=False)
    picked = lax.dot_general(
        pick, collocation[:, :PAN_DEV], (((0,), (1,)), ((), ())), preferred_element_type=jnp.float32
    ).astype(jnp.bfloat16)
    got = [send(picked, SPREAD), send(picked, SPREAD_FAR)]
    h0 = send(collocation, TRADE)
    cspair = send(pair_tensor, CORE)
    *got, h0 = lax.optimization_barrier((*got, h0))
    parts = [(a[:64], send(a, CORE)[64:]) for a in got]
    block = jnp.stack([jnp.where(c == 0, jnp.concatenate([a, b]), jnp.concatenate([b, a])) for a, b in parts])
    ring = jnp.concatenate([block, send(block, z_step(1)), send(block, z_step(-1)), send(block, z_step(2))])

    h1, h2 = send(h0, x_step(1)), send(h0, x_step(-1))
    y1, y2 = send(ring, y_step(1)), send(ring, y_step(-1))
    h1, h2, y1, y2, cspair = lax.optimization_barrier((h1, h2, y1, y2, cspair))
    h3 = send(h1, x_step(1))
    y3, y4 = send(y1[:4], y_step(1)), send(y2[4:], y_step(-1))
    h = [h0, h1, h2]
    g = [send(a, CORE) for a in h]
    shapes = ((512, 1536), jnp.float32), ((4, 8, 128, 256), jnp.bfloat16)
    gram, blocks = call(first_kernel, shapes, [], 1_800_000_000, *h, *g, ring, y1, y2)
    h3, y3, y4, gram = lax.optimization_barrier((h3, y3, y4, gram))
    h.append(h3)
    g.append(send(h3, CORE))
    shapes = (((512, 128), jnp.float32),)
    scratch = [pltpu.VMEM((8, 128, 256), jnp.bfloat16)]
    (part,) = call(last_kernel, shapes, scratch, 1_600_000_000, gram, blocks, *h, *g, pair_tensor, cspair, y3, y4)
    parts = lax.all_to_all(part.reshape(32, 16, 128), ("yh", "yl", "z"), 0, 0)
    return parts.sum(0)


def solution(mesh):
    return jax.shard_map(
        on_device,
        mesh=Mesh(mesh.devices.reshape(SIZES), AXES),
        in_specs=(P(("yh", "x"), ("yl", "z", "c")), P(("yl", "z", "c"), None)),
        out_specs=P(AXES, None),
        check_vma=False,
    )
```

```python
import jax
import jax.numpy as jnp
import numpy as np
from jax import lax
from jax.experimental import pallas as pl
from jax.experimental.pallas import tpu as pltpu
from jax.sharding import Mesh, PartitionSpec as P

PAN_DEV = 128
AXES = ("yh", "x", "yl", "z", "c")
SIZES = (2, 4, 2, 8, 2)
TILE = 512


def perm_of(move, only=lambda yh, c: True):
    pairs = []
    for s in range(256):
        yh, x, yl, z, c = (int(i) for i in np.unravel_index(s, SIZES))
        if only(yh, c):
            x, y, z, c = move(x, 2 * yh + yl, z, c)
            y = y % 4
            pairs.append((s, int(np.ravel_multi_index((y // 2, x % 4, y % 2, z % 8, c), SIZES))))
    return pairs


def is_own(y, c):
    return c == y // 2


def own(yh, c):
    return c == yh


CORE = perm_of(lambda x, y, z, c: (x, y, z, 1 - c))
SPREAD, SPREAD_FAR = (perm_of(lambda x, y, z, c: (z // 2, y, 2 * x + z % 2 + d, c)) for d in (0, 4))
TRADE = perm_of(lambda x, y, z, c: (x, y, z, c) if is_own(y, c) else (x, y + 2, z, 1 - c))


def x_step(d):
    return perm_of(lambda x, y, z, c: (x + d if c == 0 else x - d, y, z, c))


def z_step(d):
    return perm_of(lambda x, y, z, c: (x, y, z + d if c == 0 else z - d, c))


def y_step(d):
    return perm_of(lambda x, y, z, c: (x, y + d if c == 0 else y - d, z, c))


def send(a, perm):
    return lax.ppermute(a, AXES, perm)


def picker():
    m = np.zeros((2, 4, 2, 16, 2, 4, 16), np.float32)
    for c in range(2):
        for r in range(2):
            for j in range(4):
                for i in range(16):
                    m[c, j, c ^ r, i, r, j, i] = 1
    return m.reshape(2, 128, 128)


def place(blocks, ref, first=0):
    z, c = lax.axis_index("z"), lax.axis_index("c")
    side = 2 * c - 1
    for i in range(ref.shape[0]):
        off = (0, side, -side, 2 * side)[(first + i) // 2] + 4 * (i % 2)
        blocks[lax.rem(z + off + 8, 8)] = ref[i]


def first_kernel(h0, h1, h2, g0, g1, g2, *rest):
    *panel, out, blocks = rest
    yh, x, yl, c = (lax.axis_index(a) for a in ("yh", "x", "yl", "c"))
    side = 2 * c - 1
    for dy, ref in zip((0, side, -side), panel):
        place(blocks.at[lax.rem(2 * yh + yl + dy + 4, 4)], ref)

    def product(whole, partial, sign):
        @pl.loop(0, out.shape[1] // TILE)
        def _(t):
            at = pl.ds(pl.multiple_of(t * TILE, TILE), TILE)
            gram, more = 0, 0
            for dx, cols, others in zip((0, sign * side, -sign * side), whole, partial):
                z2 = 2 * lax.rem(x + dx + 4, 4)
                rows = blocks[pl.ds(2 * yh, 2), pl.ds(z2, 2)].reshape(512, 256)
                gram += jnp.dot(rows, cols[:, at], preferred_element_type=jnp.float32)
                z2 = 2 * lax.rem(x - dx + 4, 4)
                rows = blocks[2 * (1 - yh) + 1 - yl, pl.ds(z2, 2)].reshape(256, 256)
                more += jnp.dot(rows, others[:, at], preferred_element_type=jnp.float32)
            out[:, at] = gram
            out[pl.ds(pl.multiple_of((1 - yl) * 256, 256), 256), at] += more

    @pl.when(c == yh)
    def _():
        product((h0, h1, h2), (g0, g1, g2), 1)

    @pl.when(c != yh)
    def _():
        product((g0, g1, g2), (h0, h1, h2), -1)


def last_kernel(gram, blocks, h0, h1, h2, h3, g0, g1, g2, g3, pair, cspair, y3, y4, out, last):
    yh, x, yl, c = (lax.axis_index(a) for a in ("yh", "x", "yl", "c"))
    side = 2 * c - 1
    place(last, y3)
    place(last, y4, 4)
    out[...] = jnp.zeros_like(out)
    z2 = 2 * lax.rem(x + 2, 4)

    def product(whole, partial, weights, sign):
        @pl.loop(0, gram.shape[1] // TILE)
        def _(t):
            at = pl.ds(pl.multiple_of(t * TILE, TILE), TILE)
            here, there = (pl.ds(pl.multiple_of(r * 256, 256), 256) for r in (yl, 1 - yl))

            def add(values, rows, cols):
                return values + jnp.dot(rows.reshape(256, 256), cols[:, at], preferred_element_type=jnp.float32)

            def contract(rows, values):
                squared = (values * values).astype(jnp.bfloat16)
                out[rows, :] += jnp.dot(squared, weights[at, :], preferred_element_type=jnp.float32)

            values = add(gram[there, at], blocks[2 * yh + 1 - yl, pl.ds(z2, 2)], whole)
            contract(there, add(values, blocks[2 * (1 - yh) + 1 - yl, pl.ds(z2, 2)], partial[3]))
            values = add(gram[here, at], blocks[2 * yh + yl, pl.ds(z2, 2)], whole)
            for dx, cols in zip((0, sign * side, -sign * side, 2), partial):
                values = add(values, last[pl.ds(2 * lax.rem(x + dx + 4, 4), 2)], cols)
            contract(here, values)

    @pl.when(c == yh)
    def _():
        product(h3, (g0, g1, g2, g3), pair, -1)

    @pl.when(c != yh)
    def _():
        product(g3, (h0, h1, h2, h3), cspair, 1)


def call(kernel, shapes, scratch, flops, *operands):
    return pl.pallas_call(
        kernel,
        out_shape=[jax.ShapeDtypeStruct(*shape) for shape in shapes],
        in_specs=[pl.BlockSpec(memory_space=pltpu.VMEM)] * len(operands),
        out_specs=[pl.BlockSpec(memory_space=pltpu.VMEM)] * len(shapes),
        scratch_shapes=scratch,
        compiler_params=pltpu.CompilerParams(vmem_limit_bytes=24 * 2**20),
        cost_estimate=pl.CostEstimate(flops=flops, bytes_accessed=9_000_000, transcendentals=0),
    )(*operands)


def on_device(collocation, pair_tensor):
    c = lax.axis_index("c")

    pick = lax.dynamic_index_in_dim(jnp.asarray(picker(), jnp.bfloat16), c, keepdims=False)
    picked = lax.dot_general(
        pick, collocation[:, :PAN_DEV], (((0,), (1,)), ((), ())), preferred_element_type=jnp.float32
    ).astype(jnp.bfloat16)
    got = [send(picked, SPREAD), send(picked, SPREAD_FAR)]
    h0 = send(collocation, TRADE)
    cspair = send(pair_tensor, CORE)
    *got, h0 = lax.optimization_barrier((*got, h0))
    parts = [(a[:64], send(a, CORE)[64:]) for a in got]
    block = jnp.stack([jnp.where(c == 0, jnp.concatenate([a, b]), jnp.concatenate([b, a])) for a, b in parts])
    z1, z2, z3 = (send(block, z_step(d)) for d in (1, -1, 2))
    ring = jnp.concatenate([block, z1, z2, z3])

    h1, h2 = send(h0, x_step(1)), send(lax.optimization_barrier((h0, z1))[0], x_step(-1))
    y1, y2 = send(ring, y_step(1)), send(ring, y_step(-1))
    h3 = send(lax.optimization_barrier((h1, ring))[0], x_step(1))
    h2, y1, y2, cspair = lax.optimization_barrier((h2, y1, y2, cspair))
    y3, y4 = send(y1[:4], y_step(1)), send(y2[4:], y_step(-1))
    h = [h0, h1, h2]
    g = [send(a, CORE) for a in h]
    shapes = ((512, 1536), jnp.float32), ((4, 8, 128, 256), jnp.bfloat16)
    gram, blocks = call(first_kernel, shapes, [], 1_800_000_000, *h, *g, ring, y1, y2)
    y3, y4, gram = lax.optimization_barrier((y3, y4, gram))
    h.append(h3)
    g.append(send(h3, CORE))
    shapes = (((512, 128), jnp.float32),)
    scratch = [pltpu.VMEM((8, 128, 256), jnp.bfloat16)]
    (part,) = call(last_kernel, shapes, scratch, 1_600_000_000, gram, blocks, *h, *g, pair_tensor, cspair, y3, y4)
    parts = lax.all_to_all(part.reshape(32, 16, 128), ("yh", "yl", "z"), 0, 0)
    return parts.sum(0)


def solution(mesh):
    return jax.shard_map(
        on_device,
        mesh=Mesh(mesh.devices.reshape(SIZES), AXES),
        in_specs=(P(("yh", "x"), ("yl", "z", "c")), P(("yl", "z", "c"), None)),
        out_specs=P(AXES, None),
        check_vma=False,
    )
```

```python
import jax
import jax.numpy as jnp
import numpy as np
from jax import lax
from jax.experimental import pallas as pl
from jax.experimental.pallas import tpu as pltpu
from jax.sharding import Mesh, PartitionSpec as P

PAN_DEV = 128
AXES = ("yh", "x", "yl", "z", "c")
SIZES = (2, 4, 2, 8, 2)
TILE = 512


def perm_of(move, only=lambda yh, c: True):
    pairs = []
    for s in range(256):
        yh, x, yl, z, c = (int(i) for i in np.unravel_index(s, SIZES))
        if only(yh, c):
            x, y, z, c = move(x, 2 * yh + yl, z, c)
            y = y % 4
            pairs.append((s, int(np.ravel_multi_index((y // 2, x % 4, y % 2, z % 8, c), SIZES))))
    return pairs


def is_own(y, c):
    return c == y // 2


def own(yh, c):
    return c == yh


CORE = perm_of(lambda x, y, z, c: (x, y, z, 1 - c))
SPREAD, SPREAD_FAR = (perm_of(lambda x, y, z, c: (z // 2, y, 2 * x + z % 2 + d, c)) for d in (0, 4))
TRADE = perm_of(lambda x, y, z, c: (x, y + 2, z, 1 - c), lambda yh, c: c != yh)


def x_step(d):
    return perm_of(lambda x, y, z, c: (x + d if c == 0 else x - d, y, z, c))


def z_step(d):
    return perm_of(lambda x, y, z, c: (x, y, z + d if c == 0 else z - d, c))


def y_step(d):
    return perm_of(lambda x, y, z, c: (x, y + d if c == 0 else y - d, z, c))


def send(a, perm):
    return lax.ppermute(a, AXES, perm)


def picker():
    m = np.zeros((2, 4, 2, 16, 2, 4, 16), np.float32)
    for c in range(2):
        for r in range(2):
            for j in range(4):
                for i in range(16):
                    m[c, j, c ^ r, i, r, j, i] = 1
    return m.reshape(2, 128, 128)


def place(blocks, ref, first=0):
    z, c = lax.axis_index("z"), lax.axis_index("c")
    side = 2 * c - 1
    for i in range(ref.shape[0]):
        off = (0, side, -side, 2 * side)[(first + i) // 2] + 4 * (i % 2)
        blocks[lax.rem(z + off + 8, 8)] = ref[i]


def first_kernel(h0, h1, h2, g0, g1, g2, *rest):
    *panel, out, blocks = rest
    yh, x, yl, c = (lax.axis_index(a) for a in ("yh", "x", "yl", "c"))
    side = 2 * c - 1
    for dy, ref in zip((0, side, -side), panel):
        place(blocks.at[lax.rem(2 * yh + yl + dy + 4, 4)], ref)

    def product(whole, partial, sign):
        @pl.loop(0, out.shape[1] // TILE)
        def _(t):
            at = pl.ds(pl.multiple_of(t * TILE, TILE), TILE)
            gram, more = 0, 0
            for dx, cols, others in zip((0, sign * side, -sign * side), whole, partial):
                z2 = 2 * lax.rem(x + dx + 4, 4)
                rows = blocks[pl.ds(2 * yh, 2), pl.ds(z2, 2)].reshape(512, 256)
                gram += jnp.dot(rows, cols[:, at], preferred_element_type=jnp.float32)
                z2 = 2 * lax.rem(x - dx + 4, 4)
                rows = blocks[2 * (1 - yh) + 1 - yl, pl.ds(z2, 2)].reshape(256, 256)
                more += jnp.dot(rows, others[:, at], preferred_element_type=jnp.float32)
            out[:, at] = gram
            out[pl.ds(pl.multiple_of((1 - yl) * 256, 256), 256), at] += more

    @pl.when(c == yh)
    def _():
        product((h0, h1, h2), (g0, g1, g2), 1)

    @pl.when(c != yh)
    def _():
        product((g0, g1, g2), (h0, h1, h2), -1)


def last_kernel(gram, blocks, h0, h1, h2, h3, g0, g1, g2, g3, pair, cspair, y3, y4, out, last):
    yh, x, yl, c = (lax.axis_index(a) for a in ("yh", "x", "yl", "c"))
    side = 2 * c - 1
    place(last, y3)
    place(last, y4, 4)
    out[...] = jnp.zeros_like(out)
    z2 = 2 * lax.rem(x + 2, 4)

    def product(whole, partial, weights, sign):
        @pl.loop(0, gram.shape[1] // TILE)
        def _(t):
            at = pl.ds(pl.multiple_of(t * TILE, TILE), TILE)
            here, there = (pl.ds(pl.multiple_of(r * 256, 256), 256) for r in (yl, 1 - yl))

            def add(values, rows, cols):
                return values + jnp.dot(rows.reshape(256, 256), cols[:, at], preferred_element_type=jnp.float32)

            def contract(rows, values):
                squared = (values * values).astype(jnp.bfloat16)
                out[rows, :] += jnp.dot(squared, weights[at, :], preferred_element_type=jnp.float32)

            values = add(gram[there, at], blocks[2 * yh + 1 - yl, pl.ds(z2, 2)], whole)
            contract(there, add(values, blocks[2 * (1 - yh) + 1 - yl, pl.ds(z2, 2)], partial[3]))
            values = add(gram[here, at], blocks[2 * yh + yl, pl.ds(z2, 2)], whole)
            for dx, cols in zip((0, sign * side, -sign * side, 2), partial):
                values = add(values, last[pl.ds(2 * lax.rem(x + dx + 4, 4), 2)], cols)
            contract(here, values)

    @pl.when(c == yh)
    def _():
        product(h3, (g0, g1, g2, g3), pair, -1)

    @pl.when(c != yh)
    def _():
        product(g3, (h0, h1, h2, h3), cspair, 1)


def call(kernel, shapes, scratch, flops, *operands):
    return pl.pallas_call(
        kernel,
        out_shape=[jax.ShapeDtypeStruct(*shape) for shape in shapes],
        in_specs=[pl.BlockSpec(memory_space=pltpu.VMEM)] * len(operands),
        out_specs=[pl.BlockSpec(memory_space=pltpu.VMEM)] * len(shapes),
        scratch_shapes=scratch,
        compiler_params=pltpu.CompilerParams(vmem_limit_bytes=24 * 2**20),
        cost_estimate=pl.CostEstimate(flops=flops, bytes_accessed=9_000_000, transcendentals=0),
    )(*operands)


def on_device(collocation, pair_tensor):
    c = lax.axis_index("c")

    pick = lax.dynamic_index_in_dim(jnp.asarray(picker(), jnp.bfloat16), c, keepdims=False)
    picked = lax.dot_general(
        pick, collocation[:, :PAN_DEV], (((0,), (1,)), ((), ())), preferred_element_type=jnp.float32
    ).astype(jnp.bfloat16)
    got = [send(picked, SPREAD), send(picked, SPREAD_FAR)]
    h0 = send(collocation, TRADE)
    cspair = send(pair_tensor, CORE)
    *got, h0 = lax.optimization_barrier((*got, h0))
    h0 = jnp.where(c == lax.axis_index("yh"), collocation, h0)
    parts = [(a[:64], send(a, CORE)[64:]) for a in got]
    block = jnp.stack([jnp.where(c == 0, jnp.concatenate([a, b]), jnp.concatenate([b, a])) for a, b in parts])
    z1, z2, z3 = (send(block, z_step(d)) for d in (1, -1, 2))
    ring = jnp.concatenate([block, z1, z2, z3])

    h1, h2 = send(h0, x_step(1)), send(lax.optimization_barrier((h0, z1))[0], x_step(-1))
    y1, y2 = send(ring, y_step(1)), send(ring, y_step(-1))
    h3 = send(lax.optimization_barrier((h1, ring))[0], x_step(1))
    h2, y1, y2, cspair = lax.optimization_barrier((h2, y1, y2, cspair))
    y3, y4 = send(y1[:4], y_step(1)), send(y2[4:], y_step(-1))
    h = [h0, h1, h2]
    g = [send(a, CORE) for a in h]
    shapes = ((512, 1536), jnp.float32), ((4, 8, 128, 256), jnp.bfloat16)
    gram, blocks = call(first_kernel, shapes, [], 1_800_000_000, *h, *g, ring, y1, y2)
    y3, y4, gram = lax.optimization_barrier((y3, y4, gram))
    h.append(h3)
    g.append(send(h3, CORE))
    shapes = (((512, 128), jnp.float32),)
    scratch = [pltpu.VMEM((8, 128, 256), jnp.bfloat16)]
    (part,) = call(last_kernel, shapes, scratch, 1_600_000_000, gram, blocks, *h, *g, pair_tensor, cspair, y3, y4)
    parts = lax.all_to_all(part.reshape(32, 16, 128), ("yh", "yl", "z"), 0, 0)
    return parts.sum(0)


def solution(mesh):
    return jax.shard_map(
        on_device,
        mesh=Mesh(mesh.devices.reshape(SIZES), AXES),
        in_specs=(P(("yh", "x"), ("yl", "z", "c")), P(("yl", "z", "c"), None)),
        out_specs=P(AXES, None),
        check_vma=False,
    )
```

```python
import jax
import jax.numpy as jnp
import numpy as np
from jax import lax
from jax.experimental import pallas as pl
from jax.experimental.pallas import tpu as pltpu
from jax.sharding import Mesh, PartitionSpec as P

PAN_DEV = 128
AXES = ("yh", "x", "yl", "z", "c")
SIZES = (2, 4, 2, 8, 2)
TILE = 512


def perm_of(move, only=lambda yh, c: True):
    pairs = []
    for s in range(256):
        yh, x, yl, z, c = (int(i) for i in np.unravel_index(s, SIZES))
        if only(yh, c):
            x, y, z, c = move(x, 2 * yh + yl, z, c)
            y = y % 4
            pairs.append((s, int(np.ravel_multi_index((y // 2, x % 4, y % 2, z % 8, c), SIZES))))
    return pairs


def is_own(y, c):
    return c == y // 2


def own(yh, c):
    return c == yh


CORE = perm_of(lambda x, y, z, c: (x, y, z, 1 - c))
SPREAD, SPREAD_FAR = (perm_of(lambda x, y, z, c: (z // 2, y, 2 * x + z % 2 + d, c)) for d in (0, 4))
TRADE = perm_of(lambda x, y, z, c: (x, y, z, c) if is_own(y, c) else (x, y + 2, z, 1 - c))


def x_step(d):
    return perm_of(lambda x, y, z, c: (x + d if c == 0 else x - d, y, z, c))


def z_step(d):
    return perm_of(lambda x, y, z, c: (x, y, z + d if c == 0 else z - d, c))


def y_step(d):
    return perm_of(lambda x, y, z, c: (x, y + d if c == 0 else y - d, z, c))


def send(a, perm):
    return lax.ppermute(a, AXES, perm)


def picker():
    m = np.zeros((2, 4, 2, 16, 2, 4, 16), np.float32)
    for c in range(2):
        for r in range(2):
            for j in range(4):
                for i in range(16):
                    m[c, j, c ^ r, i, r, j, i] = 1
    return m.reshape(2, 128, 128)


def place(blocks, ref, first=0):
    z, c = lax.axis_index("z"), lax.axis_index("c")
    side = 2 * c - 1
    for i in range(ref.shape[0]):
        off = (0, side, -side, 2 * side)[(first + i) // 2] + 4 * (i % 2)
        blocks[lax.rem(z + off + 8, 8)] = ref[i]


def first_kernel(h0, h1, h2, g0, g1, g2, *rest):
    *panel, out, blocks = rest
    yh, x, yl, c = (lax.axis_index(a) for a in ("yh", "x", "yl", "c"))
    side = 2 * c - 1
    for dy, ref in zip((0, side, -side), panel):
        place(blocks.at[lax.rem(2 * yh + yl + dy + 4, 4)], ref)

    def product(whole, partial, sign):
        @pl.loop(0, out.shape[1] // TILE)
        def _(t):
            at = pl.ds(pl.multiple_of(t * TILE, TILE), TILE)
            gram, more = 0, 0
            for dx, cols, others in zip((0, sign * side, -sign * side), whole, partial):
                z2 = 2 * lax.rem(x + dx + 4, 4)
                rows = blocks[pl.ds(2 * yh, 2), pl.ds(z2, 2)].reshape(512, 256)
                gram += jnp.dot(rows, cols[:, at], preferred_element_type=jnp.float32)
                z2 = 2 * lax.rem(x - dx + 4, 4)
                rows = blocks[2 * (1 - yh) + 1 - yl, pl.ds(z2, 2)].reshape(256, 256)
                more += jnp.dot(rows, others[:, at], preferred_element_type=jnp.float32)
            out[:, at] = gram
            out[pl.ds(pl.multiple_of((1 - yl) * 256, 256), 256), at] += more

    @pl.when(c == yh)
    def _():
        product((h0, h1, h2), (g0, g1, g2), 1)

    @pl.when(c != yh)
    def _():
        product((g0, g1, g2), (h0, h1, h2), -1)


def last_kernel(gram, blocks, h0, h1, h2, h3, g0, g1, g2, g3, pair, cspair, y3, y4, out, last):
    yh, x, yl, c = (lax.axis_index(a) for a in ("yh", "x", "yl", "c"))
    side = 2 * c - 1
    place(last, y3)
    place(last, y4, 4)
    out[...] = jnp.zeros_like(out)
    z2 = 2 * lax.rem(x + 2, 4)

    def product(whole, partial, weights, sign):
        @pl.loop(0, gram.shape[1] // TILE)
        def _(t):
            at = pl.ds(pl.multiple_of(t * TILE, TILE), TILE)
            here, there = (pl.ds(pl.multiple_of(r * 256, 256), 256) for r in (yl, 1 - yl))

            def add(values, rows, cols):
                return values + jnp.dot(rows.reshape(256, 256), cols[:, at], preferred_element_type=jnp.float32)

            def contract(rows, values):
                squared = (values * values).astype(jnp.bfloat16)
                out[rows, :] += jnp.dot(squared, weights[at, :], preferred_element_type=jnp.float32)

            values = add(gram[there, at], blocks[2 * yh + 1 - yl, pl.ds(z2, 2)], whole)
            contract(there, add(values, blocks[2 * (1 - yh) + 1 - yl, pl.ds(z2, 2)], partial[3]))
            values = add(gram[here, at], blocks[2 * yh + yl, pl.ds(z2, 2)], whole)
            for dx, cols in zip((0, sign * side, -sign * side, 2), partial):
                values = add(values, last[pl.ds(2 * lax.rem(x + dx + 4, 4), 2)], cols)
            contract(here, values)

    @pl.when(c == yh)
    def _():
        product(h3, (g0, g1, g2, g3), pair, -1)

    @pl.when(c != yh)
    def _():
        product(g3, (h0, h1, h2, h3), cspair, 1)


def call(kernel, shapes, scratch, flops, *operands):
    return pl.pallas_call(
        kernel,
        out_shape=[jax.ShapeDtypeStruct(*shape) for shape in shapes],
        in_specs=[pl.BlockSpec(memory_space=pltpu.VMEM)] * len(operands),
        out_specs=[pl.BlockSpec(memory_space=pltpu.VMEM)] * len(shapes),
        scratch_shapes=scratch,
        compiler_params=pltpu.CompilerParams(vmem_limit_bytes=24 * 2**20),
        cost_estimate=pl.CostEstimate(flops=flops, bytes_accessed=9_000_000, transcendentals=0),
    )(*operands)


def on_device(collocation, pair_tensor):
    c = lax.axis_index("c")

    pick = lax.dynamic_index_in_dim(jnp.asarray(picker(), jnp.bfloat16), c, keepdims=False)
    picked = lax.dot_general(
        pick, collocation[:, :PAN_DEV], (((0,), (1,)), ((), ())), preferred_element_type=jnp.float32
    ).astype(jnp.bfloat16)
    got = [send(picked, SPREAD), send(picked, SPREAD_FAR)]
    h0 = send(collocation, TRADE)
    cspair = send(pair_tensor, CORE)
    *got, h0 = lax.optimization_barrier((*got, h0))
    parts = [(a[:64], send(a, CORE)[64:]) for a in got]
    block = jnp.stack([jnp.where(c == 0, jnp.concatenate([a, b]), jnp.concatenate([b, a])) for a, b in parts])
    z1, z2, z3 = (send(block, z_step(d)) for d in (1, -1, 2))
    ring = jnp.concatenate([block, z1, z2, z3])

    h1, h2 = send(h0, x_step(1)), send(lax.optimization_barrier((h0, z1, z2))[0], x_step(-1))
    y1, y2 = send(ring, y_step(1)), send(ring, y_step(-1))
    h3 = send(lax.optimization_barrier((h1, ring))[0], x_step(1))
    h2, y1, y2, cspair = lax.optimization_barrier((h2, y1, y2, cspair))
    y3, y4 = send(y1[:4], y_step(1)), send(y2[4:], y_step(-1))
    h = [h0, h1, h2]
    g = [send(a, CORE) for a in h]
    shapes = ((512, 1536), jnp.float32), ((4, 8, 128, 256), jnp.bfloat16)
    gram, blocks = call(first_kernel, shapes, [], 1_800_000_000, *h, *g, ring, y1, y2)
    y3, y4, gram = lax.optimization_barrier((y3, y4, gram))
    h.append(h3)
    g.append(send(h3, CORE))
    shapes = (((512, 128), jnp.float32),)
    scratch = [pltpu.VMEM((8, 128, 256), jnp.bfloat16)]
    (part,) = call(last_kernel, shapes, scratch, 1_600_000_000, gram, blocks, *h, *g, pair_tensor, cspair, y3, y4)
    parts = lax.all_to_all(part.reshape(32, 16, 128), ("yh", "yl", "z"), 0, 0)
    return parts.sum(0)


def solution(mesh):
    return jax.shard_map(
        on_device,
        mesh=Mesh(mesh.devices.reshape(SIZES), AXES),
        in_specs=(P(("yh", "x"), ("yl", "z", "c")), P(("yl", "z", "c"), None)),
        out_specs=P(AXES, None),
        check_vma=False,
    )
```
